32 devices in a mesh: ctx: 4 (over x, core), fsdp: 8 (over z, y).
Axes of the slice: x: 2, y: 2, z: 4, core: 2. Of those that a mesh axis runs over, the one named last changes fastest.
Arguments:
- tokens: bfloat16 [8, 4, 2, 448, 576], P('fsdp', 'ctx'), may hold values from -6 to 6
- positions: int32 [8, 4, 2, 448], P('fsdp', 'ctx'), may hold values from 0 to 3583, as said below
- attn_gain: bfloat16 [576], P('fsdp'), may hold values from 0.099609375 to 1.8984375
- w_query: bfloat16 [576, 576], P('fsdp'), may hold values from -0.25 to 0.25
- w_key: bfloat16 [576, 192], P('fsdp'), may hold values from -0.25 to 0.25
- w_value: bfloat16 [576, 192], P('fsdp'), may hold values from -0.25 to 0.25
- w_out: bfloat16 [576, 576], P('fsdp'), may hold values from -4 to 4
- mlp_gain: bfloat16 [576], P('fsdp'), may hold values from 0.099609375 to 1.8984375
- w_gate: bfloat16 [576, 1536], P('fsdp'), may hold values from -0.25 to 0.25
- w_up: bfloat16 [576, 1536], P('fsdp'), may hold values from -0.25 to 0.25
- w_down: bfloat16 [1536, 576], P('fsdp'), may hold values from -0.15625 to 0.15625
- cotangent: bfloat16 [8, 4, 2, 448, 576], P('fsdp', 'ctx'), may hold values from -6 to 6
Outputs:
- block_out: float32 [8, 4, 2, 448, 576], P('fsdp', 'ctx')
- tokens_grad: float32 [8, 4, 2, 448, 576], P('fsdp', 'ctx')
- attn_gain_grad: float32 [576], P('fsdp')
- query_grad: float32 [576, 576], P('fsdp')
- key_grad: float32 [576, 192], P('fsdp')
- value_grad: float32 [576, 192], P('fsdp')
- out_grad: float32 [576, 576], P('fsdp')
- mlp_gain_grad: float32 [576], P('fsdp')
- gate_grad: float32 [576, 1536], P('fsdp')
- up_grad: float32 [576, 1536], P('fsdp')
- down_grad: float32 [1536, 576], P('fsdp')
The draws below stay inside these ranges and needn't reach their ends.
Inputs may be any that keep to these rules, and one draw needn't show every extreme that they name: `positions`: each sequence is a pack of documents: a token's position counts the tokens before it in its own document, in natural order, and is 0 at each document's first token and at the sequence's first token; at least one sequence of each draw is a single document.
All inputs are finite; a program needn't handle non-finite values.
Results may differ from the reference program's by a relative error of at most 0.02.
Values may be sent and summed in bfloat16 or wider, within the bound.
A program may use at most 384 MiB of HBM per device.

```python
import jax
import jax.numpy as jnp
from jax import lax

D = 576
FF = 1536
HD = 64
LEN = 3584
SEQS = 8
BLK = 448
QW = 576
KVW = 192
N_CTX = 4


def draw_positions(key, part):
    key = jax.random.fold_in(key, 11)
    start_key, pick_key = jax.random.split(key)
    chance = jax.random.randint(start_key, (SEQS, LEN), 0, max(LEN // 4, 2))
    single = jax.random.randint(pick_key, (), 0, SEQS)
    seq_ids = jnp.arange(SEQS, dtype=jnp.int32)[:, None]
    col_ids = jnp.arange(LEN, dtype=jnp.int32)[None, :]
    starts = (chance == 0) & (seq_ids != single) | (col_ids == 0)
    marked = jnp.where(starts, col_ids, 0)
    begins = lax.cummax(marked, axis=1)
    natural_pos = col_ids - begins
    blocks = natural_pos.reshape(SEQS, LEN // BLK, BLK)
    half_count = LEN // BLK // 2
    return jnp.stack([blocks[:, :half_count], blocks[:, half_count:][:, ::-1]], axis=2).astype(jnp.int32)


def steps_of(key, dims, pieces, smallest, top_value):
    level = 1.0
    for axis_at, blocks in pieces:
        heights = jax.random.uniform(jax.random.fold_in(jax.random.fold_in(key, 6), axis_at), (blocks,), jnp.float32, smallest / len(pieces), top_value / len(pieces))
        level = level * jnp.repeat(jnp.exp(heights), dims[axis_at] // blocks).reshape((-1,) + (1,) * (len(dims) - 1 - axis_at))
    return level


def bell_draw(key, shape, deviation, most, cuts=(), kind=jnp.bfloat16):
    result = deviation * jax.random.normal(key, shape, jnp.float32)
    if cuts:
        result = result * steps_of(key, shape, cuts, -0.22, 0.18)
    return jnp.clip(result, -most, most).astype(kind)


def setup_inputs(seed: int = 0) -> dict:
    key_list = jax.random.split(jax.random.key(seed), 13)
    return {
        "tokens": bell_draw(key_list[0], (SEQS, N_CTX, 2, BLK, D), 1.0, 6.0, ((0, 8), (1, 4))),
        "positions": draw_positions(jax.random.fold_in(key_list[12], 71), 0),
        "attn_gain": jnp.clip(1.0 + 0.18 * jax.random.normal(key_list[2], (D,), jnp.float32), 0.099609375, 1.8984375).astype(jnp.bfloat16),
        "w_query": bell_draw(key_list[3], (D, QW), D ** -0.5, 0.25, ((0, 8),)),
        "w_key": bell_draw(key_list[4], (D, KVW), D ** -0.5, 0.25, ((0, 8),)),
        "w_value": bell_draw(key_list[5], (D, KVW), D ** -0.5, 0.25, ((0, 8),)),
        "w_out": bell_draw(key_list[6], (QW, D), (max(1, 16 * QW // LEN)) ** -0.5, 4.0, ((0, 8),)),
        "mlp_gain": jnp.clip(1.0 + 0.18 * jax.random.normal(key_list[7], (D,), jnp.float32), 0.099609375, 1.8984375).astype(jnp.bfloat16),
        "w_gate": bell_draw(key_list[8], (D, FF), D ** -0.5, 0.25, ((0, 8),)),
        "w_up": bell_draw(key_list[9], (D, FF), D ** -0.5, 0.25, ((0, 8),)),
        "w_down": bell_draw(key_list[10], (FF, D), FF ** -0.5, 0.15625, ((0, 8),)),
        "cotangent": bell_draw(key_list[11], (SEQS, N_CTX, 2, BLK, D), 1.0, 6.0, ((0, 8), (1, 4))),
    }


@jax.custom_vjp
def low(v):
    return lax.optimization_barrier(v.astype(jnp.bfloat16)).astype(jnp.float32)

@jax.custom_vjp
def low_back(v):
    return v

def low_keep(v):
    return (low(v), None)

def low_pass(kept, grad):
    return (grad,)

def back_keep(v):
    return (v, None)

def back_low(kept, grad):
    return (low(grad),)
low.defvjp(low_keep, low_pass)
low_back.defvjp(back_keep, back_low)
NORM_EPS = 1e-05
ROPE_BASE = 100000.0
ATTN_SCALE = 0.125
MASKED = -1e+30
PRECISE = lax.Precision.HIGHEST

def matmul(left, right):
    return jnp.dot(left, right, preferred_element_type=jnp.float32, precision=PRECISE)

def natural(blocks):
    front_blocks = blocks[:, :, 0]
    back_blocks = blocks[:, ::-1, 1]
    joined = jnp.concatenate([front_blocks, back_blocks], axis=1)
    return joined.reshape((joined.shape[0], joined.shape[1] * joined.shape[2]) + joined.shape[3:])

def to_dealt(rows_nat):
    blocks = rows_nat.reshape((rows_nat.shape[0], LEN // BLK, BLK) + rows_nat.shape[2:])
    half_count = LEN // BLK // 2
    return jnp.stack([blocks[:, :half_count], blocks[:, half_count:][:, ::-1]], axis=2)

def rope_tables(positions):
    exponents = jnp.arange(HD // 2, dtype=jnp.float32) * (2.0 / HD)
    frequency = jnp.exp(-exponents * jnp.log(jnp.float32(ROPE_BASE)))
    angles = positions.astype(jnp.float32)[:, None] * frequency[None, :]
    return (jnp.cos(angles)[:, None, :], jnp.sin(angles)[:, None, :])

def rotate(field, cosines, sine_vals):
    front_half = field[..., :HD // 2]
    back_half = field[..., HD // 2:]
    return jnp.concatenate([front_half * cosines - back_half * sine_vals, back_half * cosines + front_half * sine_vals], axis=-1)

def rms_scale(field):
    return lax.rsqrt(lax.optimization_barrier(jnp.mean(field * field, axis=-1, keepdims=True)) + NORM_EPS)

def attend_rows(query_blk, first_row, key_rows, value_rows):
    scores = jnp.einsum('qhd,khd->hqk', query_blk, key_rows, precision=PRECISE) * ATTN_SCALE
    scores = low_back(scores)
    row_ids = first_row + jnp.arange(query_blk.shape[0], dtype=jnp.int32)
    col_ids = jnp.arange(key_rows.shape[0], dtype=jnp.int32)
    allowed = row_ids[:, None] >= col_ids[None, :]
    scores = jnp.where(allowed[None], scores, MASKED)
    row_max = lax.optimization_barrier(jnp.max(scores, axis=-1, keepdims=True))
    exponent = jnp.exp(scores - row_max)
    attn_probs = exponent / lax.optimization_barrier(jnp.sum(exponent, axis=-1, keepdims=True))
    return jnp.einsum('hqk,khd->qhd', low(attn_probs), value_rows, precision=PRECISE)

def attention(queries, key_rows, value_rows):
    length = queries.shape[0]
    num_heads = queries.shape[1]
    group_size = num_heads // key_rows.shape[1]
    key_full = jnp.repeat(key_rows, group_size, axis=1)
    value_full = jnp.repeat(value_rows, group_size, axis=1)
    block_rows = 512 if length % 512 == 0 else length
    block_count = length // block_rows
    starts = jnp.arange(block_count, dtype=jnp.int32) * block_rows
    blocked = queries.reshape(block_count, block_rows, num_heads, HD)
    checked = jax.checkpoint(attend_rows)
    results = lax.map(lambda element: checked(element[0], element[1], key_full, value_full), (blocked, starts))
    return results.reshape(length, num_heads * HD)

def block_layer(layer_in, positions, weights):
    attn_gain, w_query, w_key, w_value, w_out, mlp_gain, w_gate, w_up, w_down = weights
    length = layer_in.shape[0]
    num_heads = w_query.shape[1] // HD
    kv_heads = w_key.shape[1] // HD
    cosines, sine_vals = rope_tables(positions)
    normed = low(layer_in * rms_scale(layer_in) * attn_gain)
    queries = low_back(matmul(normed, w_query)).reshape(length, num_heads, HD)
    key_rows = low_back(matmul(normed, w_key)).reshape(length, kv_heads, HD)
    value_rows = low_back(low(matmul(normed, w_value))).reshape(length, kv_heads, HD)
    queries = low(rotate(queries, cosines, sine_vals))
    key_rows = low(rotate(key_rows, cosines, sine_vals))
    attended = low_back(low(attention(queries, key_rows, value_rows)))
    hidden = layer_in + low_back(matmul(attended, w_out))
    second = low(hidden * rms_scale(hidden) * mlp_gain)
    gate_proj = low_back(matmul(second, w_gate))
    up_proj = low_back(matmul(second, w_up))
    inner_act = low(jax.nn.silu(gate_proj) * up_proj)
    return hidden + low_back(matmul(inner_act, w_down))

def reference(tokens, positions, attn_gain, w_query, w_key, w_value, w_out, mlp_gain, w_gate, w_up, w_down, cotangent):
    seq_in = natural(tokens.astype(jnp.float32))
    seq_pos = natural(positions)
    seq_cot = natural(cotangent.astype(jnp.float32))
    weights = tuple((weight.astype(jnp.float32) for weight in (attn_gain, w_query, w_key, w_value, w_out, mlp_gain, w_gate, w_up, w_down)))

    def whole_pass(inputs, *params):

        def one_step(carried, element):
            return (carried, block_layer(element[0], element[1], params))
        return lax.scan(one_step, None, (inputs, seq_pos))[1]
    results, pullback = jax.vjp(whole_pass, seq_in, *weights)
    gradients = pullback(seq_cot)
    return (to_dealt(results), to_dealt(gradients[0]), gradients[1], gradients[2], gradients[3], gradients[4], gradients[5], gradients[6], gradients[7], gradients[8], gradients[9])
```

```python
import jax
import jax.numpy as jnp
from jax import lax
from jax.experimental import pallas as pl
from jax.experimental.pallas import tpu as pltpu
from jax.sharding import PartitionSpec as P

HD = 64


NORM_EPS = 1e-05
ROPE_BASE = 100000.0
ATTN_SCALE = 0.125
MASKED = -1e30


def rope_tables(positions):
    exponents = jnp.arange(HD // 2, dtype=jnp.float32) * (2.0 / HD)
    frequency = jnp.exp(-exponents * jnp.log(jnp.float32(ROPE_BASE)))
    angles = positions.astype(jnp.float32)[:, None] * frequency[None, :]
    return (jnp.cos(angles)[:, None, :], jnp.sin(angles)[:, None, :])


def rotate(field, cosines, sine_vals):
    front_half = field[..., : HD // 2]
    back_half = field[..., HD // 2 :]
    return jnp.concatenate(
        [
            front_half * cosines - back_half * sine_vals,
            back_half * cosines + front_half * sine_vals,
        ],
        axis=-1,
    )


def rms_scale(field):
    return lax.rsqrt(jnp.mean(field * field, axis=-1, keepdims=True) + NORM_EPS)


def dot_nt(left, right):
    return lax.dot_general(
        left, right, (((1,), (1,)), ((), ())), preferred_element_type=jnp.float32
    )


def dot_nn(left, right):
    return jnp.dot(left, right, preferred_element_type=jnp.float32)


def dealt_index(natural, block_count):
    half = block_count // 2
    return jnp.where(natural < half, 2 * natural, 2 * (block_count - 1 - natural) + 1)


def attention_forward_kernel(
    block_ref, within_ref, query_ref, key_ref, value_t_ref, out_ref, lse_ref, acc, top, total
):
    block_count, block_len = key_ref.shape[2], key_ref.shape[3]
    mine = block_ref[pl.program_id(2)]
    query = query_ref[0, 0, 0]

    at = dealt_index(mine, block_count)
    scores = dot_nt(key_ref[0, 0, at], query)
    key_ids = lax.broadcasted_iota(jnp.int32, scores.shape, 0)
    scores = jnp.where(key_ids <= within_ref[...], scores, MASKED)
    row_max = jnp.max(scores, axis=0, keepdims=True)
    exponent = jnp.exp(scores - row_max)
    top[...] = row_max
    total[...] = jnp.sum(exponent, axis=0, keepdims=True)
    acc[...] = dot_nn(value_t_ref[0, 0, at], exponent.astype(jnp.bfloat16))

    @pl.loop(0, mine)
    def _(step):
        at = dealt_index(step, block_count)
        scores = dot_nt(key_ref[0, 0, at], query)
        old_max = top[...]
        row_max = jnp.maximum(old_max, jnp.max(scores, axis=0, keepdims=True))
        exponent = jnp.exp(scores - row_max)
        shrink = jnp.exp(old_max - row_max)
        top[...] = row_max
        total[...] = total[...] * shrink + jnp.sum(exponent, axis=0, keepdims=True)
        acc[...] = acc[...] * shrink + dot_nn(
            value_t_ref[0, 0, at], exponent.astype(jnp.bfloat16)
        )

    out_ref[0, 0, 0] = acc[...] / total[...]
    lse_ref[0, 0, 0] = top[...] + jnp.log(total[...])


def attention_backward_kernel(
    block_ref,
    within_ref,
    query_ref,
    grad_ref,
    lse_ref,
    delta_ref,
    key_ref,
    key_t_ref,
    value_ref,
    query_out,
    key_out,
    value_out,
):
    block_count, block_len = key_ref.shape[2], key_ref.shape[3]
    mine = block_ref[pl.program_id(2)]
    query = query_ref[0, 0, 0]
    grad = grad_ref[0, 0, 0]
    lse = lse_ref[0, 0, 0]
    delta = delta_ref[0, 0, 0]

    @pl.when(pl.program_id(2) == 0)
    def _():
        key_out[...] = jnp.zeros_like(key_out)
        value_out[...] = jnp.zeros_like(value_out)

    def one_block(natural, diagonal):
        at = dealt_index(natural, block_count)
        scores = dot_nt(key_ref[0, 0, at], query)
        probs = jnp.exp(scores - lse)
        if diagonal:
            key_ids = lax.broadcasted_iota(jnp.int32, scores.shape, 0)
            probs = jnp.where(key_ids <= within_ref[...], probs, 0.0)
        prob_grad = dot_nt(value_ref[0, 0, at], grad)
        score_grad = (probs * (prob_grad - delta)).astype(jnp.bfloat16)
        value_out[0, 0, at] += dot_nn(probs.astype(jnp.bfloat16), grad)
        key_out[0, 0, at] += dot_nn(score_grad, query)
        return dot_nn(key_t_ref[0, 0, at], score_grad)

    query_out[0, 0, 0] = one_block(mine, True)

    @pl.loop(0, mine)
    def _(step):
        query_out[0, 0, 0] += one_block(step, False)


def attention_specs(seqs, groups, rows, block_count, block_len):
    smem = pl.BlockSpec(memory_space=pltpu.SMEM)
    within = pl.BlockSpec((1, rows), lambda s, g, b: (0, 0))

    def own(*dims):
        return pl.BlockSpec((1, 1, 1) + dims, lambda s, g, b: (s, g, b, 0, 0))

    def shared(*dims):
        return pl.BlockSpec((1, 1, block_count) + dims, lambda s, g, b: (s, g, 0, 0, 0))

    return smem, within, own, shared


def attention_forward(blocks, within, query, key, value_t):
    seqs, groups, pair, rows, _ = query.shape
    block_count, block_len = key.shape[2], key.shape[3]
    smem, within_spec, own, shared = attention_specs(seqs, groups, rows, block_count, block_len)
    pairs = seqs * groups * pair * rows * block_len * block_count * 9 // 16
    return pl.pallas_call(
        attention_forward_kernel,
        grid=(seqs, groups, pair),
        out_shape=(
            jax.ShapeDtypeStruct((seqs, groups, pair, HD, rows), jnp.float32),
            jax.ShapeDtypeStruct((seqs, groups, pair, 1, rows), jnp.float32),
        ),
        in_specs=[smem, within_spec, own(rows, HD), shared(block_len, HD), shared(HD, block_len)],
        out_specs=(own(HD, rows), own(1, rows)),
        scratch_shapes=[
            pltpu.VMEM((HD, rows), jnp.float32),
            pltpu.VMEM((1, rows), jnp.float32),
            pltpu.VMEM((1, rows), jnp.float32),
        ],
        compiler_params=pltpu.CompilerParams(vmem_limit_bytes=48 * 1024 * 1024),
        cost_estimate=pl.CostEstimate(
            flops=4 * HD * pairs, bytes_accessed=8 * query.size, transcendentals=pairs
        ),
        name="attention_forward",
    )(blocks, within, query, key, value_t)


def attention_backward(blocks, within, query, grad, lse, delta, key, key_t, value):
    seqs, groups, pair, rows, _ = query.shape
    block_count, block_len = key.shape[2], key.shape[3]
    smem, within_spec, own, shared = attention_specs(seqs, groups, rows, block_count, block_len)
    pairs = seqs * groups * pair * rows * block_len * block_count * 9 // 16
    return pl.pallas_call(
        attention_backward_kernel,
        grid=(seqs, groups, pair),
        out_shape=(
            jax.ShapeDtypeStruct((seqs, groups, pair, HD, rows), jnp.float32),
            jax.ShapeDtypeStruct((seqs, groups, block_count, block_len, HD), jnp.float32),
            jax.ShapeDtypeStruct((seqs, groups, block_count, block_len, HD), jnp.float32),
        ),
        in_specs=[
            smem,
            within_spec,
            own(rows, HD),
            own(rows, HD),
            own(1, rows),
            own(1, rows),
            shared(block_len, HD),
            shared(HD, block_len),
            shared(block_len, HD),
        ],
        out_specs=(own(HD, rows), shared(block_len, HD), shared(block_len, HD)),
        compiler_params=pltpu.CompilerParams(vmem_limit_bytes=56 * 1024 * 1024),
        cost_estimate=pl.CostEstimate(
            flops=10 * HD * pairs, bytes_accessed=20 * query.size, transcendentals=pairs
        ),
        name="attention_backward",
    )(blocks, within, query, grad, lse, delta, key, key_t, value)


def rows_by_cols(left, right):
    return jnp.einsum("rd,rf->df", left, right, preferred_element_type=jnp.float32)


def times_transpose(left, right):
    return jnp.einsum("rf,df->rd", left, right, preferred_element_type=jnp.float32)


def local(
    tokens,
    positions,
    attn_gain,
    w_query,
    w_key,
    w_value,
    w_out,
    mlp_gain,
    w_gate,
    w_up,
    w_down,
    cotangent,
):
    seq_count = tokens.shape[0]
    block_len = tokens.shape[3]
    model_width = tokens.shape[4]
    pair_len = 2 * block_len
    row_total = seq_count * pair_len
    ctx_count = lax.axis_size("ctx")
    ctx_id = lax.axis_index("ctx")
    layer_in = tokens.reshape(row_total, model_width).astype(jnp.float32)
    cosines, sine_vals = rope_tables(positions.reshape(row_total))
    block_total = 2 * ctx_count
    own_blocks = jnp.stack([ctx_id, block_total - 1 - ctx_id]).astype(jnp.int32)
    weights_full = (
        lax.all_gather(attn_gain, "fsdp", axis=0, tiled=True),
        lax.all_gather(w_query, "fsdp", axis=0, tiled=True),
        lax.all_gather(w_key, "fsdp", axis=0, tiled=True),
        lax.all_gather(w_value, "fsdp", axis=0, tiled=True),
        lax.all_gather(w_out, "fsdp", axis=0, tiled=True),
        lax.all_gather(mlp_gain, "fsdp", axis=0, tiled=True),
        lax.all_gather(w_gate, "fsdp", axis=0, tiled=True),
        lax.all_gather(w_up, "fsdp", axis=0, tiled=True),
        lax.all_gather(w_down, "fsdp", axis=0, tiled=True),
    )
    gain_one, query_w, key_w, value_w, out_w, gain_two, gate_w, up_w, down_w = weights_full
    num_heads = query_w.shape[1] // HD
    kv_heads = key_w.shape[1] // HD
    group_size = num_heads // kv_heads
    query_width = num_heads * HD
    kv_width = kv_heads * HD
    inv_one = rms_scale(layer_in)
    normed = (layer_in * inv_one * gain_one.astype(jnp.float32)).astype(jnp.bfloat16)
    query_raw = jnp.dot(normed, query_w, preferred_element_type=jnp.float32).reshape(
        row_total, num_heads, HD
    )
    key_raw = jnp.dot(normed, key_w, preferred_element_type=jnp.float32).reshape(
        row_total, kv_heads, HD
    )
    queries = rotate(query_raw, cosines, sine_vals).astype(jnp.bfloat16)
    key_rows = rotate(key_raw, cosines, sine_vals).astype(jnp.bfloat16)
    value_rows = jnp.dot(normed, value_w, preferred_element_type=jnp.float32).astype(jnp.bfloat16)
    key_value = jnp.concatenate(
        [key_rows.reshape(row_total, kv_width), value_rows], axis=-1
    ).reshape(seq_count, pair_len, 2 * kv_width)

    def by_group(rows):
        split = rows.reshape(seq_count, 2, block_len, kv_heads, group_size, HD)
        return split.transpose(0, 3, 1, 4, 2, 5).reshape(
            seq_count, kv_heads, 2, group_size * block_len, HD
        )

    def from_group(rows_t):
        split = rows_t.reshape(seq_count, kv_heads, 2, HD, group_size, block_len)
        return split.transpose(0, 2, 5, 1, 4, 3).reshape(row_total, num_heads, HD)

    within = jnp.tile(jnp.arange(block_len, dtype=jnp.int32), group_size)[None, :]
    query_groups = by_group(queries * jnp.bfloat16(ATTN_SCALE))
    kv_all = lax.all_gather(key_value, "ctx", axis=1, tiled=True).reshape(
        seq_count, block_total, block_len, 2, kv_heads, HD
    )
    keys_all = kv_all[:, :, :, 0].transpose(0, 3, 1, 2, 4)
    values_all = kv_all[:, :, :, 1].transpose(0, 3, 1, 2, 4)
    keys_t = kv_all[:, :, :, 0].transpose(0, 3, 1, 4, 2)
    values_t = kv_all[:, :, :, 1].transpose(0, 3, 1, 4, 2)
    attended_t, log_sums = attention_forward(own_blocks, within, query_groups, keys_all, values_t)
    attended = from_group(attended_t).reshape(row_total, query_width)
    attended_flat = attended.astype(jnp.bfloat16)
    hidden = layer_in + jnp.dot(attended_flat, out_w, preferred_element_type=jnp.float32)
    inv_two = rms_scale(hidden)
    second = (hidden * inv_two * gain_two.astype(jnp.float32)).astype(jnp.bfloat16)
    gate_proj = jnp.dot(second, gate_w, preferred_element_type=jnp.float32)
    up_proj = jnp.dot(second, up_w, preferred_element_type=jnp.float32)
    inner_act = (jax.nn.silu(gate_proj) * up_proj).astype(jnp.bfloat16)
    block_out = hidden + jnp.dot(inner_act, down_w, preferred_element_type=jnp.float32)
    grad_out = cotangent.reshape(row_total, model_width)
    down_wgrad = rows_by_cols(inner_act, grad_out)
    inner_grad = times_transpose(grad_out, down_w)
    sigmoid_gate = jax.nn.sigmoid(gate_proj)
    silu_val = gate_proj * sigmoid_gate
    silu_slope = sigmoid_gate * (1.0 + gate_proj * (1.0 - sigmoid_gate))
    gate_back = (inner_grad * up_proj * silu_slope).astype(jnp.bfloat16)
    up_back = (inner_grad * silu_val).astype(jnp.bfloat16)
    gate_wgrad = rows_by_cols(second, gate_back)
    up_wgrad = rows_by_cols(second, up_back)
    second_grad = times_transpose(gate_back, gate_w) + times_transpose(up_back, up_w)
    gain_two_grad = jnp.sum(second_grad * hidden * inv_two, axis=0)
    scaled_two = second_grad * gain_two.astype(jnp.float32)
    hidden_grad = (
        grad_out.astype(jnp.float32)
        + inv_two * scaled_two
        - hidden * inv_two**3 * jnp.mean(scaled_two * hidden, axis=-1, keepdims=True)
    )
    hidden_low = hidden_grad.astype(jnp.bfloat16)
    out_wgrad = rows_by_cols(attended_flat, hidden_low)
    attended_grad = times_transpose(hidden_low, out_w).astype(jnp.bfloat16)
    delta = jnp.sum(
        (attended * attended_grad.astype(jnp.float32)).reshape(row_total, num_heads, HD), axis=-1
    )
    delta_groups = (
        delta.reshape(seq_count, 2, block_len, kv_heads, group_size)
        .transpose(0, 3, 1, 4, 2)
        .reshape(seq_count, kv_heads, 2, 1, group_size * block_len)
    )
    query_grad_t, key_terms, value_terms = attention_backward(
        own_blocks,
        within,
        query_groups,
        by_group(attended_grad),
        log_sums,
        delta_groups,
        keys_all,
        keys_t,
        values_all,
    )
    kv_terms = (
        jnp.stack([key_terms, value_terms], axis=1)
        .transpose(0, 3, 4, 1, 2, 5)
        .reshape(seq_count, block_total * block_len, 2 * kv_width)
    )
    kv_grad_all = lax.psum_scatter(
        kv_terms.astype(jnp.bfloat16), "ctx", scatter_dimension=1, tiled=True
    ).astype(jnp.float32)
    query_grad_all = from_group(query_grad_t) * ATTN_SCALE
    query_back = (
        rotate(query_grad_all, cosines, -sine_vals)
        .reshape(row_total, query_width)
        .astype(jnp.bfloat16)
    )
    key_back = (
        rotate(kv_grad_all[:, :, :kv_width].reshape(row_total, kv_heads, HD), cosines, -sine_vals)
        .reshape(row_total, kv_width)
        .astype(jnp.bfloat16)
    )
    value_back = kv_grad_all[:, :, kv_width:].reshape(row_total, kv_width).astype(jnp.bfloat16)
    query_wgrad = rows_by_cols(normed, query_back)
    key_wgrad = rows_by_cols(normed, key_back)
    value_wgrad = rows_by_cols(normed, value_back)
    normed_grad = (
        times_transpose(query_back, query_w)
        + times_transpose(key_back, key_w)
        + times_transpose(value_back, value_w)
    )
    gain_one_grad = jnp.sum(normed_grad * layer_in * inv_one, axis=0)
    scaled_one = normed_grad * gain_one.astype(jnp.float32)
    input_grad = (
        hidden_grad
        + inv_one * scaled_one
        - layer_in * inv_one**3 * jnp.mean(scaled_one * layer_in, axis=-1, keepdims=True)
    )
    shares = (
        lax.psum_scatter(
            gain_one_grad.astype(jnp.bfloat16), "fsdp", scatter_dimension=0, tiled=True
        ).astype(jnp.float32),
        lax.psum_scatter(
            query_wgrad.astype(jnp.bfloat16), "fsdp", scatter_dimension=0, tiled=True
        ).astype(jnp.float32),
        lax.psum_scatter(
            key_wgrad.astype(jnp.bfloat16), "fsdp", scatter_dimension=0, tiled=True
        ).astype(jnp.float32),
        lax.psum_scatter(
            value_wgrad.astype(jnp.bfloat16), "fsdp", scatter_dimension=0, tiled=True
        ).astype(jnp.float32),
        lax.psum_scatter(
            out_wgrad.astype(jnp.bfloat16), "fsdp", scatter_dimension=0, tiled=True
        ).astype(jnp.float32),
        lax.psum_scatter(
            gain_two_grad.astype(jnp.bfloat16), "fsdp", scatter_dimension=0, tiled=True
        ).astype(jnp.float32),
        lax.psum_scatter(
            gate_wgrad.astype(jnp.bfloat16), "fsdp", scatter_dimension=0, tiled=True
        ).astype(jnp.float32),
        lax.psum_scatter(
            up_wgrad.astype(jnp.bfloat16), "fsdp", scatter_dimension=0, tiled=True
        ).astype(jnp.float32),
        lax.psum_scatter(
            down_wgrad.astype(jnp.bfloat16), "fsdp", scatter_dimension=0, tiled=True
        ).astype(jnp.float32),
    )
    totals = (
        lax.psum(shares[0].astype(jnp.bfloat16), "ctx").astype(jnp.float32),
        lax.psum(shares[1].astype(jnp.bfloat16), "ctx").astype(jnp.float32),
        lax.psum(shares[2].astype(jnp.bfloat16), "ctx").astype(jnp.float32),
        lax.psum(shares[3].astype(jnp.bfloat16), "ctx").astype(jnp.float32),
        lax.psum(shares[4].astype(jnp.bfloat16), "ctx").astype(jnp.float32),
        lax.psum(shares[5].astype(jnp.bfloat16), "ctx").astype(jnp.float32),
        lax.psum(shares[6].astype(jnp.bfloat16), "ctx").astype(jnp.float32),
        lax.psum(shares[7].astype(jnp.bfloat16), "ctx").astype(jnp.float32),
        lax.psum(shares[8].astype(jnp.bfloat16), "ctx").astype(jnp.float32),
    )
    return (
        block_out.reshape(tokens.shape),
        input_grad.reshape(tokens.shape),
        totals[0],
        totals[1],
        totals[2],
        totals[3],
        totals[4],
        totals[5],
        totals[6],
        totals[7],
        totals[8],
    )


def solution(mesh):
    placed = (
        P("fsdp", "ctx", None, None, None),
        P("fsdp", "ctx", None, None),
        P("fsdp"),
        P("fsdp", None),
        P("fsdp", None),
        P("fsdp", None),
        P("fsdp", None),
        P("fsdp"),
        P("fsdp", None),
        P("fsdp", None),
        P("fsdp", None),
        P("fsdp", "ctx", None, None, None),
    )
    return jax.shard_map(
        local,
        mesh=mesh,
        in_specs=placed,
        out_specs=(
            P("fsdp", "ctx", None, None, None),
            P("fsdp", "ctx", None, None, None),
            P("fsdp"),
            P("fsdp", None),
            P("fsdp", None),
            P("fsdp", None),
            P("fsdp", None),
            P("fsdp"),
            P("fsdp", None),
            P("fsdp", None),
            P("fsdp", None),
        ),
        check_vma=False,
    )
```

```python
import jax
import jax.numpy as jnp
from jax import lax
from jax.experimental import pallas as pl
from jax.experimental.pallas import tpu as pltpu
from jax.sharding import PartitionSpec as P

HD = 64


NORM_EPS = 1e-05
ROPE_BASE = 100000.0
ATTN_SCALE = 0.125
MASKED = -1e30


def rope_tables(positions):
    exponents = jnp.arange(HD // 2, dtype=jnp.float32) * (2.0 / HD)
    frequency = jnp.exp(-exponents * jnp.log(jnp.float32(ROPE_BASE)))
    angles = positions.astype(jnp.float32)[:, None] * frequency[None, :]
    return (jnp.cos(angles)[:, None, :], jnp.sin(angles)[:, None, :])


def rotate(field, cosines, sine_vals):
    front_half = field[..., : HD // 2]
    back_half = field[..., HD // 2 :]
    return jnp.concatenate(
        [
            front_half * cosines - back_half * sine_vals,
            back_half * cosines + front_half * sine_vals,
        ],
        axis=-1,
    )


def rms_scale(field):
    return lax.rsqrt(jnp.mean(field * field, axis=-1, keepdims=True) + NORM_EPS)


def dot_nt(left, right):
    return lax.dot_general(
        left, right, (((1,), (1,)), ((), ())), preferred_element_type=jnp.float32
    )


def dot_nn(left, right):
    return jnp.dot(left, right, preferred_element_type=jnp.float32)


def dealt_index(natural, block_count):
    half = block_count // 2
    return jnp.where(natural < half, 2 * natural, 2 * (block_count - 1 - natural) + 1)


def attention_forward_kernel(
    block_ref, within_ref, query_ref, key_ref, value_t_ref, out_ref, lse_ref, acc, top, total
):
    block_count, block_len = key_ref.shape[2], key_ref.shape[3]
    mine = block_ref[pl.program_id(2)]
    query = query_ref[0, 0, 0]

    at = dealt_index(mine, block_count)
    scores = dot_nt(key_ref[0, 0, at], query)
    key_ids = lax.broadcasted_iota(jnp.int32, scores.shape, 0)
    scores = jnp.where(key_ids <= within_ref[...], scores, MASKED)
    row_max = jnp.max(scores, axis=0, keepdims=True)
    exponent = jnp.exp(scores - row_max)
    top[...] = row_max
    total[...] = jnp.sum(exponent, axis=0, keepdims=True)
    acc[...] = dot_nn(value_t_ref[0, 0, at], exponent.astype(jnp.bfloat16))

    @pl.loop(0, mine)
    def _(step):
        at = dealt_index(step, block_count)
        scores = dot_nt(key_ref[0, 0, at], query)
        old_max = top[...]
        row_max = jnp.maximum(old_max, jnp.max(scores, axis=0, keepdims=True))
        exponent = jnp.exp(scores - row_max)
        shrink = jnp.exp(old_max - row_max)
        top[...] = row_max
        total[...] = total[...] * shrink + jnp.sum(exponent, axis=0, keepdims=True)
        acc[...] = acc[...] * shrink + dot_nn(
            value_t_ref[0, 0, at], exponent.astype(jnp.bfloat16)
        )

    out_ref[0, 0, 0] = acc[...] / total[...]
    lse_ref[0, 0, 0] = top[...] + jnp.log(total[...])


def attention_backward_kernel(
    block_ref,
    within_ref,
    query_ref,
    grad_ref,
    lse_ref,
    delta_ref,
    key_ref,
    key_t_ref,
    value_ref,
    query_out,
    key_out,
    value_out,
):
    block_count, block_len = key_ref.shape[2], key_ref.shape[3]
    mine = block_ref[pl.program_id(2)]
    query = query_ref[0, 0, 0]
    grad = grad_ref[0, 0, 0]
    lse = lse_ref[0, 0, 0]
    delta = delta_ref[0, 0, 0]

    @pl.when(pl.program_id(2) == 0)
    def _():
        key_out[...] = jnp.zeros_like(key_out)
        value_out[...] = jnp.zeros_like(value_out)

    def one_block(natural, diagonal):
        at = dealt_index(natural, block_count)
        scores = dot_nt(key_ref[0, 0, at], query)
        probs = jnp.exp(scores - lse)
        if diagonal:
            key_ids = lax.broadcasted_iota(jnp.int32, scores.shape, 0)
            probs = jnp.where(key_ids <= within_ref[...], probs, 0.0)
        prob_grad = dot_nt(value_ref[0, 0, at], grad)
        score_grad = (probs * (prob_grad - delta)).astype(jnp.bfloat16)
        value_out[0, 0, at] += dot_nn(probs.astype(jnp.bfloat16), grad)
        key_out[0, 0, at] += dot_nn(score_grad, query)
        return dot_nn(key_t_ref[0, 0, at], score_grad)

    query_out[0, 0, 0] = one_block(mine, True)

    @pl.loop(0, mine)
    def _(step):
        query_out[0, 0, 0] += one_block(step, False)


def attention_specs(seqs, groups, rows, block_count, block_len):
    smem = pl.BlockSpec(memory_space=pltpu.SMEM)
    within = pl.BlockSpec((1, rows), lambda s, g, b: (0, 0))

    def own(*dims):
        return pl.BlockSpec((1, 1, 1) + dims, lambda s, g, b: (s, g, b, 0, 0))

    def shared(*dims):
        return pl.BlockSpec((1, 1, block_count) + dims, lambda s, g, b: (s, g, 0, 0, 0))

    return smem, within, own, shared


def attention_forward(blocks, within, query, key, value_t):
    seqs, groups, pair, rows, _ = query.shape
    block_count, block_len = key.shape[2], key.shape[3]
    smem, within_spec, own, shared = attention_specs(seqs, groups, rows, block_count, block_len)
    pairs = seqs * groups * pair * rows * block_len * block_count * 9 // 16
    return pl.pallas_call(
        attention_forward_kernel,
        grid=(seqs, groups, pair),
        out_shape=(
            jax.ShapeDtypeStruct((seqs, groups, pair, HD, rows), jnp.float32),
            jax.ShapeDtypeStruct((seqs, groups, pair, 1, rows), jnp.float32),
        ),
        in_specs=[smem, within_spec, own(rows, HD), shared(block_len, HD), shared(HD, block_len)],
        out_specs=(own(HD, rows), own(1, rows)),
        scratch_shapes=[
            pltpu.VMEM((HD, rows), jnp.float32),
            pltpu.VMEM((1, rows), jnp.float32),
            pltpu.VMEM((1, rows), jnp.float32),
        ],
        compiler_params=pltpu.CompilerParams(vmem_limit_bytes=48 * 1024 * 1024),
        cost_estimate=pl.CostEstimate(
            flops=4 * HD * pairs, bytes_accessed=8 * query.size, transcendentals=pairs
        ),
        name="attention_forward",
    )(blocks, within, query, key, value_t)


def attention_backward(blocks, within, query, grad, lse, delta, key, key_t, value):
    seqs, groups, pair, rows, _ = query.shape
    block_count, block_len = key.shape[2], key.shape[3]
    smem, within_spec, own, shared = attention_specs(seqs, groups, rows, block_count, block_len)
    pairs = seqs * groups * pair * rows * block_len * block_count * 9 // 16
    return pl.pallas_call(
        attention_backward_kernel,
        grid=(seqs, groups, pair),
        out_shape=(
            jax.ShapeDtypeStruct((seqs, groups, pair, HD, rows), jnp.float32),
            jax.ShapeDtypeStruct((seqs, groups, block_count, block_len, HD), jnp.float32),
            jax.ShapeDtypeStruct((seqs, groups, block_count, block_len, HD), jnp.float32),
        ),
        in_specs=[
            smem,
            within_spec,
            own(rows, HD),
            own(rows, HD),
            own(1, rows),
            own(1, rows),
            shared(block_len, HD),
            shared(HD, block_len),
            shared(block_len, HD),
        ],
        out_specs=(own(HD, rows), shared(block_len, HD), shared(block_len, HD)),
        compiler_params=pltpu.CompilerParams(vmem_limit_bytes=56 * 1024 * 1024),
        cost_estimate=pl.CostEstimate(
            flops=10 * HD * pairs, bytes_accessed=20 * query.size, transcendentals=pairs
        ),
        name="attention_backward",
    )(blocks, within, query, grad, lse, delta, key, key_t, value)


def exchange(arr, axis, bit):
    count = lax.axis_size(axis)
    return lax.ppermute(arr, axis, [(at, at ^ (1 << bit)) for at in range(count)])


def my_bit(axis, bit):
    return lax.axis_index(axis) >> bit & 1


def bits_of(axis):
    return range(lax.axis_size(axis).bit_length() - 1)


def gather_blocks(arr, axis, dim):
    arr = jnp.expand_dims(arr, dim)
    for bit in reversed(bits_of(axis)):
        got = exchange(arr, axis, bit)
        arr = jnp.where(
            my_bit(axis, bit) == 0,
            jnp.stack([arr, got], axis=dim + 1),
            jnp.stack([got, arr], axis=dim + 1),
        )
        arr = arr.reshape(arr.shape[:dim] + (-1,) + arr.shape[dim + 2 :])
    return arr


def scatter_blocks(arr, axis, dim):
    for bit in bits_of(axis):
        halves = arr.reshape(arr.shape[:dim] + (-1, 2) + arr.shape[dim + 1 :])
        mine = my_bit(axis, bit)
        send = lax.dynamic_index_in_dim(halves, 1 - mine, dim + 1, keepdims=False)
        keep = lax.dynamic_index_in_dim(halves, mine, dim + 1, keepdims=False)
        arr = keep + exchange(send, axis, bit)
    return jnp.squeeze(arr, dim)


def take_part(arr, axis, dim, bits):
    for bit in bits:
        size = arr.shape[dim] // 2
        arr = lax.dynamic_slice_in_dim(arr, my_bit(axis, bit) * size, size, dim)
    return arr


def scatter_parts(arr, axis, dim):
    for bit in bits_of(axis):
        size = arr.shape[dim] // 2
        mine = my_bit(axis, bit)
        send = lax.dynamic_slice_in_dim(arr, (1 - mine) * size, size, dim)
        keep = lax.dynamic_slice_in_dim(arr, mine * size, size, dim)
        arr = keep + exchange(send, axis, bit)
    return arr


def gather_parts(arr, axis, dim, bits):
    for bit in reversed(bits):
        got = exchange(arr, axis, bit)
        arr = jnp.where(
            my_bit(axis, bit) == 0,
            jnp.concatenate([arr, got], axis=dim),
            jnp.concatenate([got, arr], axis=dim),
        )
    return arr


def gather_weight(shard, dim, bits):
    part = take_part(shard, "ctx", dim, bits)
    return gather_parts(gather_blocks(part, "fsdp", 0), "ctx", dim + 1, bits)


def reduce_weight(terms, dim):
    part = scatter_parts(terms.astype(jnp.bfloat16), "ctx", dim + 1)
    part = scatter_blocks(part, "fsdp", 0)
    return gather_parts(part, "ctx", dim, bits_of("ctx")).astype(jnp.float32)


def pad_to(arr, dim, multiple):
    widths = [(0, 0)] * arr.ndim
    widths[dim] = (0, -arr.shape[dim] % multiple)
    return jnp.pad(arr, widths)


def rows_by_cols(left, right):
    return jnp.einsum("rd,rf->df", left, right, preferred_element_type=jnp.float32)


def times_transpose(left, right):
    return jnp.einsum("rf,df->rd", left, right, preferred_element_type=jnp.float32)


def local(
    tokens,
    positions,
    attn_gain,
    w_query,
    w_key,
    w_value,
    w_out,
    mlp_gain,
    w_gate,
    w_up,
    w_down,
    cotangent,
):
    seq_count = tokens.shape[0]
    block_len = tokens.shape[3]
    model_width = tokens.shape[4]
    pair_len = 2 * block_len
    row_total = seq_count * pair_len
    ctx_count = lax.axis_size("ctx")
    ctx_id = lax.axis_index("ctx")
    layer_in = tokens.reshape(row_total, model_width).astype(jnp.float32)
    cosines, sine_vals = rope_tables(positions.reshape(row_total))
    block_total = 2 * ctx_count
    own_blocks = jnp.stack([ctx_id, block_total - 1 - ctx_id]).astype(jnp.int32)
    fsdp_count = lax.axis_size("fsdp")
    q_cols, k_cols, v_cols = w_query.shape[1], w_key.shape[1], w_value.shape[1]
    ff_cols = w_gate.shape[1]
    down_rows, out_rows = w_down.shape[0], w_out.shape[0]
    col_unit, row_unit = 128 * ctx_count, 8 * ctx_count
    gains = jnp.stack([attn_gain, mlp_gain], axis=1)
    first_pack = pad_to(
        jnp.concatenate([w_query, w_key, w_value, gains], axis=1), 1, col_unit
    )
    row_pack = pad_to(jnp.concatenate([w_down, w_out], axis=0), 0, row_unit)
    gate_up = jnp.concatenate([w_gate, w_up], axis=1)
    every = bits_of("ctx")
    first_full = gather_weight(first_pack, 1, every[:1]).reshape(model_width, -1)
    rows_full = gather_weight(row_pack, 0, every)
    gate_up_full = gather_weight(gate_up, 1, every).reshape(model_width, -1)
    qk_cols = q_cols + k_cols
    qkv_cols = qk_cols + v_cols
    query_w = first_full[:, :q_cols]
    key_w = first_full[:, q_cols:qk_cols]
    value_w = first_full[:, qk_cols:qkv_cols]
    gain_one = first_full[:, qkv_cols]
    gain_two = first_full[:, qkv_cols + 1]
    down_w = rows_full[:, :down_rows].reshape(fsdp_count * down_rows, -1)
    out_w = rows_full[:, down_rows : down_rows + out_rows].reshape(fsdp_count * out_rows, -1)
    gate_w, up_w = gate_up_full[:, :ff_cols], gate_up_full[:, ff_cols:]
    num_heads = query_w.shape[1] // HD
    kv_heads = key_w.shape[1] // HD
    group_size = num_heads // kv_heads
    query_width = num_heads * HD
    kv_width = kv_heads * HD
    inv_one = rms_scale(layer_in)
    normed = (layer_in * inv_one * gain_one.astype(jnp.float32)).astype(jnp.bfloat16)
    query_raw = jnp.dot(normed, query_w, preferred_element_type=jnp.float32).reshape(
        row_total, num_heads, HD
    )
    key_raw = jnp.dot(normed, key_w, preferred_element_type=jnp.float32).reshape(
        row_total, kv_heads, HD
    )
    queries = rotate(query_raw, cosines, sine_vals).astype(jnp.bfloat16)
    key_rows = rotate(key_raw, cosines, sine_vals).astype(jnp.bfloat16)
    value_rows = jnp.dot(normed, value_w, preferred_element_type=jnp.float32).astype(jnp.bfloat16)
    key_value = jnp.concatenate(
        [key_rows.reshape(row_total, kv_width), value_rows], axis=-1
    ).reshape(seq_count, pair_len, 2 * kv_width)

    def by_group(rows):
        split = rows.reshape(seq_count, 2, block_len, kv_heads, group_size, HD)
        return split.transpose(0, 3, 1, 4, 2, 5).reshape(
            seq_count, kv_heads, 2, group_size * block_len, HD
        )

    def from_group(rows_t):
        split = rows_t.reshape(seq_count, kv_heads, 2, HD, group_size, block_len)
        return split.transpose(0, 2, 5, 1, 4, 3).reshape(row_total, num_heads, HD)

    within = jnp.tile(jnp.arange(block_len, dtype=jnp.int32), group_size)[None, :]
    query_groups = by_group(queries * jnp.bfloat16(ATTN_SCALE))
    kv_all = gather_blocks(key_value, "ctx", 1).reshape(
        seq_count, block_total, block_len, 2, kv_heads, HD
    )
    keys_all = kv_all[:, :, :, 0].transpose(0, 3, 1, 2, 4)
    values_all = kv_all[:, :, :, 1].transpose(0, 3, 1, 2, 4)
    keys_t = kv_all[:, :, :, 0].transpose(0, 3, 1, 4, 2)
    values_t = kv_all[:, :, :, 1].transpose(0, 3, 1, 4, 2)
    attended_t, log_sums = attention_forward(own_blocks, within, query_groups, keys_all, values_t)
    attended = from_group(attended_t).reshape(row_total, query_width)
    attended_flat = attended.astype(jnp.bfloat16)
    hidden = layer_in + jnp.dot(attended_flat, out_w, preferred_element_type=jnp.float32)
    inv_two = rms_scale(hidden)
    second = (hidden * inv_two * gain_two.astype(jnp.float32)).astype(jnp.bfloat16)
    gate_proj = jnp.dot(second, gate_w, preferred_element_type=jnp.float32)
    up_proj = jnp.dot(second, up_w, preferred_element_type=jnp.float32)
    inner_act = (jax.nn.silu(gate_proj) * up_proj).astype(jnp.bfloat16)
    block_out = hidden + jnp.dot(inner_act, down_w, preferred_element_type=jnp.float32)
    grad_out = cotangent.reshape(row_total, model_width)
    down_wgrad = rows_by_cols(inner_act, grad_out)
    inner_grad = times_transpose(grad_out, down_w)
    sigmoid_gate = jax.nn.sigmoid(gate_proj)
    silu_val = gate_proj * sigmoid_gate
    silu_slope = sigmoid_gate * (1.0 + gate_proj * (1.0 - sigmoid_gate))
    gate_back = (inner_grad * up_proj * silu_slope).astype(jnp.bfloat16)
    up_back = (inner_grad * silu_val).astype(jnp.bfloat16)
    gate_wgrad = rows_by_cols(second, gate_back)
    up_wgrad = rows_by_cols(second, up_back)
    second_grad = times_transpose(gate_back, gate_w) + times_transpose(up_back, up_w)
    gain_two_grad = jnp.sum(second_grad * hidden * inv_two, axis=0)
    scaled_two = second_grad * gain_two.astype(jnp.float32)
    hidden_grad = (
        grad_out.astype(jnp.float32)
        + inv_two * scaled_two
        - hidden * inv_two**3 * jnp.mean(scaled_two * hidden, axis=-1, keepdims=True)
    )
    hidden_low = hidden_grad.astype(jnp.bfloat16)
    out_wgrad = rows_by_cols(attended_flat, hidden_low)
    attended_grad = times_transpose(hidden_low, out_w).astype(jnp.bfloat16)
    delta = jnp.sum(
        (attended * attended_grad.astype(jnp.float32)).reshape(row_total, num_heads, HD), axis=-1
    )
    delta_groups = (
        delta.reshape(seq_count, 2, block_len, kv_heads, group_size)
        .transpose(0, 3, 1, 4, 2)
        .reshape(seq_count, kv_heads, 2, 1, group_size * block_len)
    )
    query_grad_t, key_terms, value_terms = attention_backward(
        own_blocks,
        within,
        query_groups,
        by_group(attended_grad),
        log_sums,
        delta_groups,
        keys_all,
        keys_t,
        values_all,
    )
    kv_terms = (
        jnp.stack([key_terms, value_terms], axis=1)
        .transpose(0, 3, 4, 1, 2, 5)
        .reshape(seq_count, ctx_count, pair_len, 2 * kv_width)
    )
    kv_grad_all = scatter_blocks(kv_terms.astype(jnp.bfloat16), "ctx", 1).astype(jnp.float32)
    query_grad_all = from_group(query_grad_t) * ATTN_SCALE
    query_back = (
        rotate(query_grad_all, cosines, -sine_vals)
        .reshape(row_total, query_width)
        .astype(jnp.bfloat16)
    )
    key_back = (
        rotate(kv_grad_all[:, :, :kv_width].reshape(row_total, kv_heads, HD), cosines, -sine_vals)
        .reshape(row_total, kv_width)
        .astype(jnp.bfloat16)
    )
    value_back = kv_grad_all[:, :, kv_width:].reshape(row_total, kv_width).astype(jnp.bfloat16)
    query_wgrad = rows_by_cols(normed, query_back)
    key_wgrad = rows_by_cols(normed, key_back)
    value_wgrad = rows_by_cols(normed, value_back)
    normed_grad = (
        times_transpose(query_back, query_w)
        + times_transpose(key_back, key_w)
        + times_transpose(value_back, value_w)
    )
    gain_one_grad = jnp.sum(normed_grad * layer_in * inv_one, axis=0)
    scaled_one = normed_grad * gain_one.astype(jnp.float32)
    input_grad = (
        hidden_grad
        + inv_one * scaled_one
        - layer_in * inv_one**3 * jnp.mean(scaled_one * layer_in, axis=-1, keepdims=True)
    )
    def by_owner(wgrad):
        return wgrad.astype(jnp.bfloat16).reshape(fsdp_count, -1, wgrad.shape[1])

    gate_up_share = reduce_weight(
        jnp.concatenate([by_owner(gate_wgrad), by_owner(up_wgrad)], axis=2), 1
    )
    row_share = reduce_weight(
        pad_to(jnp.concatenate([by_owner(down_wgrad), by_owner(out_wgrad)], axis=1), 1, row_unit),
        0,
    )
    gain_terms = jnp.stack([gain_one_grad, gain_two_grad], axis=1)
    first_share = reduce_weight(
        pad_to(
            jnp.concatenate(
                [by_owner(t) for t in (query_wgrad, key_wgrad, value_wgrad, gain_terms)], axis=2
            ),
            2,
            col_unit,
        ),
        1,
    )
    totals = (
        first_share[:, qkv_cols],
        first_share[:, :q_cols],
        first_share[:, q_cols:qk_cols],
        first_share[:, qk_cols:qkv_cols],
        row_share[down_rows : down_rows + out_rows],
        first_share[:, qkv_cols + 1],
        gate_up_share[:, :ff_cols],
        gate_up_share[:, ff_cols:],
        row_share[:down_rows],
    )
    return (
        block_out.reshape(tokens.shape),
        input_grad.reshape(tokens.shape),
        totals[0],
        totals[1],
        totals[2],
        totals[3],
        totals[4],
        totals[5],
        totals[6],
        totals[7],
        totals[8],
    )


def solution(mesh):
    placed = (
        P("fsdp", "ctx", None, None, None),
        P("fsdp", "ctx", None, None),
        P("fsdp"),
        P("fsdp", None),
        P("fsdp", None),
        P("fsdp", None),
        P("fsdp", None),
        P("fsdp"),
        P("fsdp", None),
        P("fsdp", None),
        P("fsdp", None),
        P("fsdp", "ctx", None, None, None),
    )
    return jax.shard_map(
        local,
        mesh=mesh,
        in_specs=placed,
        out_specs=(
            P("fsdp", "ctx", None, None, None),
            P("fsdp", "ctx", None, None, None),
            P("fsdp"),
            P("fsdp", None),
            P("fsdp", None),
            P("fsdp", None),
            P("fsdp", None),
            P("fsdp"),
            P("fsdp", None),
            P("fsdp", None),
            P("fsdp", None),
        ),
        check_vma=False,
    )
```

```python
import jax
import jax.numpy as jnp
from jax import lax
from jax.experimental import pallas as pl
from jax.experimental.pallas import tpu as pltpu
from jax.sharding import PartitionSpec as P

HD = 64


NORM_EPS = 1e-05
ROPE_BASE = 100000.0
ATTN_SCALE = 0.125
MASKED = -1e30


def rope_tables(positions):
    exponents = jnp.arange(HD // 2, dtype=jnp.float32) * (2.0 / HD)
    frequency = jnp.exp(-exponents * jnp.log(jnp.float32(ROPE_BASE)))
    angles = positions.astype(jnp.float32)[:, None] * frequency[None, :]
    return (jnp.cos(angles)[:, None, :], jnp.sin(angles)[:, None, :])


def rotate(field, cosines, sine_vals):
    front_half = field[..., : HD // 2]
    back_half = field[..., HD // 2 :]
    return jnp.concatenate(
        [
            front_half * cosines - back_half * sine_vals,
            back_half * cosines + front_half * sine_vals,
        ],
        axis=-1,
    )


def rms_scale(field):
    return lax.rsqrt(jnp.mean(field * field, axis=-1, keepdims=True) + NORM_EPS)


def dot_nt(left, right):
    return lax.dot_general(
        left, right, (((1,), (1,)), ((), ())), preferred_element_type=jnp.float32
    )


def dot_nn(left, right):
    return jnp.dot(left, right, preferred_element_type=jnp.float32)


def dot_tn(left, right):
    return lax.dot_general(
        left, right, (((0,), (0,)), ((), ())), preferred_element_type=jnp.float32
    )


def dealt_index(natural, block_count):
    half = block_count // 2
    return jnp.where(natural < half, 2 * natural, 2 * (block_count - 1 - natural) + 1)


def attention_forward_kernel(
    block_ref, within_ref, query_ref, kv_ref, out_ref, lse_ref, acc, top, total
):
    block_count = kv_ref.shape[2]
    mine = block_ref[pl.program_id(2)]
    query = query_ref[0, 0, 0]

    at = dealt_index(mine, block_count)
    scores = dot_nt(kv_ref[0, 0, at, :, :HD], query)
    key_ids = lax.broadcasted_iota(jnp.int32, scores.shape, 0)
    scores = jnp.where(key_ids <= within_ref[...], scores, MASKED)
    row_max = jnp.max(scores, axis=0, keepdims=True)
    exponent = jnp.exp(scores - row_max)
    top[...] = row_max
    total[...] = jnp.sum(exponent, axis=0, keepdims=True)
    acc[...] = dot_tn(kv_ref[0, 0, at, :, HD:], exponent.astype(jnp.bfloat16))

    @pl.loop(0, mine)
    def _(step):
        at = dealt_index(step, block_count)
        scores = dot_nt(kv_ref[0, 0, at, :, :HD], query)
        old_max = top[...]
        row_max = jnp.maximum(old_max, jnp.max(scores, axis=0, keepdims=True))
        exponent = jnp.exp(scores - row_max)
        shrink = jnp.exp(old_max - row_max)
        top[...] = row_max
        total[...] = total[...] * shrink + jnp.sum(exponent, axis=0, keepdims=True)
        acc[...] = acc[...] * shrink + dot_tn(
            kv_ref[0, 0, at, :, HD:], exponent.astype(jnp.bfloat16)
        )

    out_ref[0, 0, 0] = acc[...] / total[...]
    lse_ref[0, 0, 0] = top[...] + jnp.log(total[...])


def attention_backward_kernel(
    block_ref,
    within_ref,
    query_ref,
    grad_ref,
    lse_ref,
    delta_ref,
    kv_ref,
    query_out,
    kv_out,
):
    block_count = kv_ref.shape[2]
    mine = block_ref[pl.program_id(2)]
    query = query_ref[0, 0, 0]
    grad = grad_ref[0, 0, 0]
    lse = lse_ref[0, 0, 0]
    delta = delta_ref[0, 0, 0]

    @pl.when(pl.program_id(2) == 0)
    def _():
        kv_out[...] = jnp.zeros_like(kv_out)

    def one_block(natural, diagonal):
        at = dealt_index(natural, block_count)
        scores = dot_nt(kv_ref[0, 0, at, :, :HD], query)
        probs = jnp.exp(scores - lse)
        if diagonal:
            key_ids = lax.broadcasted_iota(jnp.int32, scores.shape, 0)
            probs = jnp.where(key_ids <= within_ref[...], probs, 0.0)
        prob_grad = dot_nt(kv_ref[0, 0, at, :, HD:], grad)
        score_grad = (probs * (prob_grad - delta)).astype(jnp.bfloat16)
        kv_out[0, 0, at, :, HD:] += dot_nn(probs.astype(jnp.bfloat16), grad)
        kv_out[0, 0, at, :, :HD] += dot_nn(score_grad, query)
        return dot_tn(kv_ref[0, 0, at, :, :HD], score_grad)

    query_out[0, 0, 0] = one_block(mine, True)

    @pl.loop(0, mine)
    def _(step):
        query_out[0, 0, 0] += one_block(step, False)


def attention_specs(seqs, groups, rows, block_count, block_len):
    smem = pl.BlockSpec(memory_space=pltpu.SMEM)
    within = pl.BlockSpec((1, rows), lambda s, g, b: (0, 0))

    def own(*dims):
        return pl.BlockSpec((1, 1, 1) + dims, lambda s, g, b: (s, g, b, 0, 0))

    def shared(*dims):
        return pl.BlockSpec((1, 1, block_count) + dims, lambda s, g, b: (s, g, 0, 0, 0))

    return smem, within, own, shared


def attention_forward(blocks, within, query, kv):
    seqs, groups, pair, rows, _ = query.shape
    block_count, block_len = kv.shape[2], kv.shape[3]
    smem, within_spec, own, shared = attention_specs(seqs, groups, rows, block_count, block_len)
    pairs = seqs * groups * pair * rows * block_len * block_count * 9 // 16
    return pl.pallas_call(
        attention_forward_kernel,
        grid=(seqs, groups, pair),
        out_shape=(
            jax.ShapeDtypeStruct((seqs, groups, pair, HD, rows), jnp.float32),
            jax.ShapeDtypeStruct((seqs, groups, pair, 1, rows), jnp.float32),
        ),
        in_specs=[smem, within_spec, own(rows, HD), shared(block_len, 2 * HD)],
        out_specs=(own(HD, rows), own(1, rows)),
        scratch_shapes=[
            pltpu.VMEM((HD, rows), jnp.float32),
            pltpu.VMEM((1, rows), jnp.float32),
            pltpu.VMEM((1, rows), jnp.float32),
        ],
        compiler_params=pltpu.CompilerParams(vmem_limit_bytes=48 * 1024 * 1024),
        cost_estimate=pl.CostEstimate(
            flops=4 * HD * pairs, bytes_accessed=8 * query.size, transcendentals=pairs
        ),
        name="attention_forward",
    )(blocks, within, query, kv)


def attention_backward(blocks, within, query, grad, lse, delta, kv):
    seqs, groups, pair, rows, _ = query.shape
    block_count, block_len = kv.shape[2], kv.shape[3]
    smem, within_spec, own, shared = attention_specs(seqs, groups, rows, block_count, block_len)
    pairs = seqs * groups * pair * rows * block_len * block_count * 9 // 16
    return pl.pallas_call(
        attention_backward_kernel,
        grid=(seqs, groups, pair),
        out_shape=(
            jax.ShapeDtypeStruct((seqs, groups, pair, HD, rows), jnp.float32),
            jax.ShapeDtypeStruct((seqs, groups, block_count, block_len, 2 * HD), jnp.float32),
        ),
        in_specs=[
            smem,
            within_spec,
            own(rows, HD),
            own(rows, HD),
            own(1, rows),
            own(1, rows),
            shared(block_len, 2 * HD),
        ],
        out_specs=(own(HD, rows), shared(block_len, 2 * HD)),
        compiler_params=pltpu.CompilerParams(vmem_limit_bytes=56 * 1024 * 1024),
        cost_estimate=pl.CostEstimate(
            flops=10 * HD * pairs, bytes_accessed=20 * query.size, transcendentals=pairs
        ),
        name="attention_backward",
    )(blocks, within, query, grad, lse, delta, kv)


def exchange(arr, axis, bit):
    count = lax.axis_size(axis)
    return lax.ppermute(arr, axis, [(at, at ^ (1 << bit)) for at in range(count)])


def my_bit(axis, bit):
    return lax.axis_index(axis) >> bit & 1


def bits_of(axis):
    return range(lax.axis_size(axis).bit_length() - 1)


def gather_blocks(arr, axis, dim):
    arr = jnp.expand_dims(arr, dim)
    for bit in reversed(bits_of(axis)):
        got = exchange(arr, axis, bit)
        arr = jnp.where(
            my_bit(axis, bit) == 0,
            jnp.stack([arr, got], axis=dim + 1),
            jnp.stack([got, arr], axis=dim + 1),
        )
        arr = arr.reshape(arr.shape[:dim] + (-1,) + arr.shape[dim + 2 :])
    return arr


def scatter_blocks(arr, axis, dim):
    for bit in bits_of(axis):
        halves = arr.reshape(arr.shape[:dim] + (-1, 2) + arr.shape[dim + 1 :])
        mine = my_bit(axis, bit)
        send = lax.dynamic_index_in_dim(halves, 1 - mine, dim + 1, keepdims=False)
        keep = lax.dynamic_index_in_dim(halves, mine, dim + 1, keepdims=False)
        arr = keep + exchange(send, axis, bit)
    return jnp.squeeze(arr, dim)


def take_part(arr, axis, dim, bits):
    for bit in bits:
        size = arr.shape[dim] // 2
        arr = lax.dynamic_slice_in_dim(arr, my_bit(axis, bit) * size, size, dim)
    return arr


def scatter_parts(arr, axis, dim):
    for bit in bits_of(axis):
        size = arr.shape[dim] // 2
        mine = my_bit(axis, bit)
        send = lax.dynamic_slice_in_dim(arr, (1 - mine) * size, size, dim)
        keep = lax.dynamic_slice_in_dim(arr, mine * size, size, dim)
        arr = keep + exchange(send, axis, bit)
    return arr


def gather_parts(arr, axis, dim, bits):
    for bit in reversed(bits):
        got = exchange(arr, axis, bit)
        arr = jnp.where(
            my_bit(axis, bit) == 0,
            jnp.concatenate([arr, got], axis=dim),
            jnp.concatenate([got, arr], axis=dim),
        )
    return arr


def gather_weight(shard, dim, bits):
    part = take_part(shard, "ctx", dim, bits)
    return gather_parts(gather_blocks(part, "fsdp", 0), "ctx", dim + 1, bits)


def reduce_weight(terms, dim):
    part = scatter_parts(terms.astype(jnp.bfloat16), "ctx", dim + 1)
    part = scatter_blocks(part, "fsdp", 0)
    return gather_parts(part, "ctx", dim, bits_of("ctx")).astype(jnp.float32)


def pad_to(arr, dim, multiple):
    widths = [(0, 0)] * arr.ndim
    widths[dim] = (0, -arr.shape[dim] % multiple)
    return jnp.pad(arr, widths)


def rows_by_cols(left, right):
    return jnp.einsum("rd,rf->df", left, right, preferred_element_type=jnp.float32)


def times_transpose(left, right):
    return jnp.einsum("rf,df->rd", left, right, preferred_element_type=jnp.float32)


def local(
    tokens,
    positions,
    attn_gain,
    w_query,
    w_key,
    w_value,
    w_out,
    mlp_gain,
    w_gate,
    w_up,
    w_down,
    cotangent,
):
    seq_count = tokens.shape[0]
    block_len = tokens.shape[3]
    model_width = tokens.shape[4]
    pair_len = 2 * block_len
    row_total = seq_count * pair_len
    ctx_count = lax.axis_size("ctx")
    ctx_id = lax.axis_index("ctx")
    layer_in = tokens.reshape(row_total, model_width).astype(jnp.float32)
    cosines, sine_vals = rope_tables(positions.reshape(row_total))
    block_total = 2 * ctx_count
    own_blocks = jnp.stack([ctx_id, block_total - 1 - ctx_id]).astype(jnp.int32)
    fsdp_count = lax.axis_size("fsdp")
    q_cols, k_cols, v_cols = w_query.shape[1], w_key.shape[1], w_value.shape[1]
    ff_cols = w_gate.shape[1]
    down_rows, out_rows = w_down.shape[0], w_out.shape[0]
    col_unit, row_unit = 128 * ctx_count, 8 * ctx_count
    gains = jnp.stack([attn_gain, mlp_gain], axis=1)
    first_pack = pad_to(
        jnp.concatenate([w_query, w_key, w_value, gains], axis=1), 1, col_unit
    )
    row_pack = pad_to(jnp.concatenate([w_down, w_out], axis=0), 0, row_unit)
    gate_up = jnp.concatenate([w_gate, w_up], axis=1)
    every = bits_of("ctx")
    first_full = gather_weight(first_pack, 1, every[:1]).reshape(model_width, -1)
    rows_full = gather_weight(row_pack, 0, every)
    gate_up_full = gather_weight(gate_up, 1, every).reshape(model_width, -1)
    qk_cols = q_cols + k_cols
    qkv_cols = qk_cols + v_cols
    query_w = first_full[:, :q_cols]
    key_w = first_full[:, q_cols:qk_cols]
    value_w = first_full[:, qk_cols:qkv_cols]
    gain_one = first_full[:, qkv_cols]
    gain_two = first_full[:, qkv_cols + 1]
    down_w = rows_full[:, :down_rows].reshape(fsdp_count * down_rows, -1)
    out_w = rows_full[:, down_rows : down_rows + out_rows].reshape(fsdp_count * out_rows, -1)
    gate_w, up_w = gate_up_full[:, :ff_cols], gate_up_full[:, ff_cols:]
    num_heads = query_w.shape[1] // HD
    kv_heads = key_w.shape[1] // HD
    group_size = num_heads // kv_heads
    query_width = num_heads * HD
    kv_width = kv_heads * HD
    inv_one = rms_scale(layer_in)
    normed = (layer_in * inv_one * gain_one.astype(jnp.float32)).astype(jnp.bfloat16)
    query_raw = jnp.dot(normed, query_w, preferred_element_type=jnp.float32).reshape(
        row_total, num_heads, HD
    )
    key_raw = jnp.dot(normed, key_w, preferred_element_type=jnp.float32).reshape(
        row_total, kv_heads, HD
    )
    queries = rotate(query_raw, cosines, sine_vals).astype(jnp.bfloat16)
    key_rows = rotate(key_raw, cosines, sine_vals).astype(jnp.bfloat16)
    value_rows = jnp.dot(normed, value_w, preferred_element_type=jnp.float32).astype(jnp.bfloat16)
    key_value = (
        jnp.concatenate([key_rows, value_rows.reshape(row_total, kv_heads, HD)], axis=-1)
        .reshape(seq_count, 2, block_len, kv_heads, 2 * HD)
        .transpose(0, 3, 1, 2, 4)
    )

    def by_group(rows):
        split = rows.reshape(seq_count, 2, block_len, kv_heads, group_size, HD)
        return split.transpose(0, 3, 1, 4, 2, 5).reshape(
            seq_count, kv_heads, 2, group_size * block_len, HD
        )

    def from_group(rows_t):
        split = rows_t.reshape(seq_count, kv_heads, 2, HD, group_size, block_len)
        return split.transpose(0, 2, 5, 1, 4, 3).reshape(row_total, num_heads, HD)

    within = jnp.tile(jnp.arange(block_len, dtype=jnp.int32), group_size)[None, :]
    query_groups = by_group(queries * jnp.bfloat16(ATTN_SCALE))
    kv_all = gather_blocks(key_value, "ctx", 2).reshape(
        seq_count, kv_heads, block_total, block_len, 2 * HD
    )
    attended_t, log_sums = attention_forward(own_blocks, within, query_groups, kv_all)
    attended = from_group(attended_t).reshape(row_total, query_width)
    attended_flat = attended.astype(jnp.bfloat16)
    hidden = layer_in + jnp.dot(attended_flat, out_w, preferred_element_type=jnp.float32)
    inv_two = rms_scale(hidden)
    second = (hidden * inv_two * gain_two.astype(jnp.float32)).astype(jnp.bfloat16)
    gate_proj = jnp.dot(second, gate_w, preferred_element_type=jnp.float32)
    up_proj = jnp.dot(second, up_w, preferred_element_type=jnp.float32)
    inner_act = (jax.nn.silu(gate_proj) * up_proj).astype(jnp.bfloat16)
    block_out = hidden + jnp.dot(inner_act, down_w, preferred_element_type=jnp.float32)
    grad_out = cotangent.reshape(row_total, model_width)
    down_wgrad = rows_by_cols(inner_act, grad_out)
    inner_grad = times_transpose(grad_out, down_w)
    sigmoid_gate = jax.nn.sigmoid(gate_proj)
    silu_val = gate_proj * sigmoid_gate
    silu_slope = sigmoid_gate * (1.0 + gate_proj * (1.0 - sigmoid_gate))
    gate_back = (inner_grad * up_proj * silu_slope).astype(jnp.bfloat16)
    up_back = (inner_grad * silu_val).astype(jnp.bfloat16)
    gate_wgrad = rows_by_cols(second, gate_back)
    up_wgrad = rows_by_cols(second, up_back)
    second_grad = times_transpose(gate_back, gate_w) + times_transpose(up_back, up_w)
    gain_two_grad = jnp.sum(second_grad * hidden * inv_two, axis=0)
    scaled_two = second_grad * gain_two.astype(jnp.float32)
    hidden_grad = (
        grad_out.astype(jnp.float32)
        + inv_two * scaled_two
        - hidden * inv_two**3 * jnp.mean(scaled_two * hidden, axis=-1, keepdims=True)
    )
    hidden_low = hidden_grad.astype(jnp.bfloat16)
    out_wgrad = rows_by_cols(attended_flat, hidden_low)
    attended_grad = times_transpose(hidden_low, out_w).astype(jnp.bfloat16)
    delta = jnp.sum(
        (attended * attended_grad.astype(jnp.float32)).reshape(row_total, num_heads, HD), axis=-1
    )
    delta_groups = (
        delta.reshape(seq_count, 2, block_len, kv_heads, group_size)
        .transpose(0, 3, 1, 4, 2)
        .reshape(seq_count, kv_heads, 2, 1, group_size * block_len)
    )
    query_grad_t, kv_terms = attention_backward(
        own_blocks,
        within,
        query_groups,
        by_group(attended_grad),
        log_sums,
        delta_groups,
        kv_all,
    )
    kv_terms = kv_terms.astype(jnp.bfloat16).reshape(
        seq_count, kv_heads, ctx_count, 2, block_len, 2 * HD
    )
    kv_grad_all = (
        scatter_blocks(kv_terms, "ctx", 2)
        .transpose(0, 2, 3, 1, 4)
        .reshape(row_total, kv_heads, 2 * HD)
        .astype(jnp.float32)
    )
    query_grad_all = from_group(query_grad_t) * ATTN_SCALE
    query_back = (
        rotate(query_grad_all, cosines, -sine_vals)
        .reshape(row_total, query_width)
        .astype(jnp.bfloat16)
    )
    key_back = (
        rotate(kv_grad_all[:, :, :HD], cosines, -sine_vals)
        .reshape(row_total, kv_width)
        .astype(jnp.bfloat16)
    )
    value_back = kv_grad_all[:, :, HD:].reshape(row_total, kv_width).astype(jnp.bfloat16)
    query_wgrad = rows_by_cols(normed, query_back)
    key_wgrad = rows_by_cols(normed, key_back)
    value_wgrad = rows_by_cols(normed, value_back)
    normed_grad = (
        times_transpose(query_back, query_w)
        + times_transpose(key_back, key_w)
        + times_transpose(value_back, value_w)
    )
    gain_one_grad = jnp.sum(normed_grad * layer_in * inv_one, axis=0)
    scaled_one = normed_grad * gain_one.astype(jnp.float32)
    input_grad = (
        hidden_grad
        + inv_one * scaled_one
        - layer_in * inv_one**3 * jnp.mean(scaled_one * layer_in, axis=-1, keepdims=True)
    )
    def by_owner(wgrad):
        return wgrad.astype(jnp.bfloat16).reshape(fsdp_count, -1, wgrad.shape[1])

    gate_up_share = reduce_weight(
        jnp.concatenate([by_owner(gate_wgrad), by_owner(up_wgrad)], axis=2), 1
    )
    row_share = reduce_weight(
        pad_to(jnp.concatenate([by_owner(down_wgrad), by_owner(out_wgrad)], axis=1), 1, row_unit),
        0,
    )
    gain_terms = jnp.stack([gain_one_grad, gain_two_grad], axis=1)
    first_share = reduce_weight(
        pad_to(
            jnp.concatenate(
                [by_owner(t) for t in (query_wgrad, key_wgrad, value_wgrad, gain_terms)], axis=2
            ),
            2,
            col_unit,
        ),
        1,
    )
    totals = (
        first_share[:, qkv_cols],
        first_share[:, :q_cols],
        first_share[:, q_cols:qk_cols],
        first_share[:, qk_cols:qkv_cols],
        row_share[down_rows : down_rows + out_rows],
        first_share[:, qkv_cols + 1],
        gate_up_share[:, :ff_cols],
        gate_up_share[:, ff_cols:],
        row_share[:down_rows],
    )
    return (
        block_out.reshape(tokens.shape),
        input_grad.reshape(tokens.shape),
        totals[0],
        totals[1],
        totals[2],
        totals[3],
        totals[4],
        totals[5],
        totals[6],
        totals[7],
        totals[8],
    )


def solution(mesh):
    placed = (
        P("fsdp", "ctx", None, None, None),
        P("fsdp", "ctx", None, None),
        P("fsdp"),
        P("fsdp", None),
        P("fsdp", None),
        P("fsdp", None),
        P("fsdp", None),
        P("fsdp"),
        P("fsdp", None),
        P("fsdp", None),
        P("fsdp", None),
        P("fsdp", "ctx", None, None, None),
    )
    return jax.shard_map(
        local,
        mesh=mesh,
        in_specs=placed,
        out_specs=(
            P("fsdp", "ctx", None, None, None),
            P("fsdp", "ctx", None, None, None),
            P("fsdp"),
            P("fsdp", None),
            P("fsdp", None),
            P("fsdp", None),
            P("fsdp", None),
            P("fsdp"),
            P("fsdp", None),
            P("fsdp", None),
            P("fsdp", None),
        ),
        check_vma=False,
    )
```
